32 devices in a mesh: grp: 2 (over y), ep: 4 (over z), dp: 4 (over x, core).
Axes of the slice: x: 2, y: 2, z: 4, core: 2. Of those that a mesh axis runs over, the one named last changes fastest.
Arguments:
- tokens: bfloat16 [128, 7168], P(('grp', 'ep', 'dp')), parts along dimension 0, may hold values from -6 to 6
- expert_ids: int32 [128, 8], P(('grp', 'ep', 'dp')), parts along dimension 0, may hold values from 0 to 15, all different within a row; in each aligned block of 4 rows (0 to 3, 4 to 7, ...) at most 3 rows name the same one
- combine_weight: float32 [128, 8], P(('grp', 'ep', 'dp')), parts along dimension 0, may hold values from 0.1 to 1
- slot_of_expert: int32 [16], replicated, may hold values from 0 to 15, each once
- w_gate: bfloat16 [16, 7168, 2048], P('ep', None, 'dp'), may hold values from -0.0625 to 0.0625
- w_up: bfloat16 [16, 7168, 2048], P('ep', None, 'dp'), may hold values from -0.0625 to 0.0625
- w_down: bfloat16 [16, 2048, 7168], P('ep', 'dp'), may hold values from -0.125 to 0.125
Outputs:
- mixed: bfloat16 [128, 7168], P(('grp', 'ep', 'dp')), parts along dimension 0
The draws below stay inside these ranges and needn't reach their ends.
There are 2 independent parts, one for each index of `grp`. The reference program is written for one: setup_inputs(seed, part) draws one part's arguments, and reference() takes and returns one part's arrays. A program takes and returns all parts, laid end to end along the dimension named above; an argument that names none is the same for every part. Nothing has to cross between parts.
Inputs may be any that keep to these rules, and one draw needn't show every extreme that they name: `expert_ids`: among the rows of one device no expert is named by more than 3 rows. `slot_of_expert`: every stored slot serves exactly one expert.
All inputs are finite; a program needn't handle non-finite values.
Results may differ from the reference program's by a relative error of at most 0.015.
Values may be sent and summed in bfloat16 or wider, within the bound.
A program may use at most 128 MiB of HBM per device.

```python
import math
import jax
import jax.numpy as jnp
import numpy as np
from jax import lax

D = 7168
FF = 2048
TOP = 8
EXPERTS = 16
T_DEV = 4
CAP = 3
TOKENS = 64
N_DP = 4


def levels(key, extent, cuts, low, largest):
    def one(position, shards_of):
        heights = jax.random.uniform(jax.random.fold_in(jax.random.fold_in(key, 6), position), (shards_of,), jnp.float32, low / len(cuts), largest / len(cuts))
        return jnp.repeat(jnp.exp(heights), extent[position] // shards_of).reshape((-1,) + (1,) * (len(extent) - position - 1))

    loudness = one(*cuts[0])
    for cut in cuts[1:]:
        loudness = loudness * one(*cut)
    return loudness


def assign_block(key, own, number, rows, number_of, top, reach, skew):
    sequence = jax.random.permutation(key, number_of)
    crowded, ordinary = portions_of(number_of, rows * top, reach, skew, True), portions_of(number_of, rows * top, reach, skew, False)
    places = jnp.arange(number_of)

    def named(lengths, rotation):
        used = int((lengths > 0).sum())
        fixed = max(1, used // 4)
        moved = fixed + (places - fixed + rotation * (used - fixed)) % max(1, number_of - fixed)
        return jnp.zeros((number_of,), jnp.int32).at[sequence[jnp.where(places < fixed, places, moved)]].set(jnp.asarray(lengths, jnp.int32))

    lengths = jnp.where(number % 4 == 0, named(crowded, number // 4), named(ordinary, number - number // 4 - 1))
    mixed = jax.random.permutation(jax.random.fold_in(own, 3), number_of)
    giver, sink = mixed[0:number_of // 2 * 2:2], mixed[1:number_of // 2 * 2:2]
    slack = jnp.minimum(lengths[giver] - 1, reach - lengths[sink]) // 2
    slack = jnp.where((giver == sequence[0]) | (sink == sequence[0]) | (lengths[sink] == 0), 0, jnp.maximum(slack, 0))
    moved = jax.random.randint(jax.random.fold_in(own, 4), (number_of // 2,), 0, 1 << 20) % (slack + 1)
    lengths = lengths.at[giver].add(-moved).at[sink].add(moved)
    labels = jnp.searchsorted(jnp.cumsum(lengths), jnp.arange(rows * top), side="right").astype(jnp.int32)
    listing = labels.reshape(top, rows).T
    listing = listing[jax.random.permutation(jax.random.fold_in(own, 1), rows)]
    rotation = jax.random.randint(jax.random.fold_in(own, 2), (rows, 1), 0, top)
    return jnp.take_along_axis(listing, (jnp.arange(top)[None, :] + rotation) % top, axis=1)


def portions_of(count, total, bound, skew, full):
    loads = [(1 << 20) // math.isqrt(rank ** skew) + 1 for rank in range(1, count + 1)]
    largest = bound if full else min(bound, max(-(-total // count), total * loads[0] // sum(loads)))
    least = 1 if total - largest >= count - 1 else 0
    holding, spare = [largest] + [least] * (count - 1), total - largest - least * (count - 1)
    while spare > 0:
        free = [i for i in range(1, count) if holding[i] < largest] or [i for i in range(1, count) if holding[i] < bound]
        mass, budget = sum([loads[i] for i in free]), spare
        for i in free:
            addition = min(bound - holding[i], max(1, budget * loads[i] // mass), spare)
            holding[i] = holding[i] + addition
            spare = spare - addition
    return np.array(holding)


def bell_draw(key, dims, deviation, limit, pieces=(), held_as=jnp.bfloat16):
    values = deviation * jax.random.normal(key, dims, jnp.float32)
    if pieces:
        values = values * levels(key, dims, pieces, -0.22, 0.18)
    return jnp.clip(values, -limit, limit).astype(held_as)


def setup_inputs(seed: int = 0, part: int = 0) -> dict:
    arg_keys = jax.random.split(jax.random.key(seed), 8)
    own_keys = jax.random.split(jax.random.fold_in(arg_keys[7], part), 8)
    tokens = bell_draw(own_keys[0], (TOKENS, D), 1.0, 6.0, ((0, 16),))
    expert_ids_keys = jax.random.split(jax.random.fold_in(own_keys[1], 1), TOKENS // T_DEV)
    expert_ids_turns = jax.random.permutation(jax.random.fold_in(own_keys[1], 3), TOKENS // T_DEV)
    expert_ids = jax.vmap(lambda own, number: assign_block(jax.random.fold_in(own_keys[1], 2), own, number, T_DEV, EXPERTS, TOP, CAP, 2))(expert_ids_keys, expert_ids_turns).reshape((TOKENS, TOP))
    combine_weight = jnp.clip(jnp.exp(math.log(1.0) - 2.3025851 * jax.random.uniform(own_keys[2], (TOKENS, TOP), jnp.float32) ** levels(own_keys[2], (TOKENS, TOP), ((0, 16),), -0.2, 0.2)), 0.1, 1.0)
    slot_of_expert = jax.random.permutation(arg_keys[3], EXPERTS).astype(jnp.int32)
    w_gate = bell_draw(arg_keys[4], (EXPERTS, D, FF), D ** -0.5, 0.0625, ((0, 4), (2, 4)))
    w_up = bell_draw(arg_keys[5], (EXPERTS, D, FF), D ** -0.5, 0.0625, ((0, 4), (2, 4)))
    w_down = bell_draw(arg_keys[6], (EXPERTS, FF, D), FF ** -0.5, 0.125, ((0, 4), (1, 4)))
    return dict(tokens=tokens, expert_ids=expert_ids, combine_weight=combine_weight, slot_of_expert=slot_of_expert, w_gate=w_gate, w_up=w_up, w_down=w_down)


def round_trip(values):
    return lax.optimization_barrier(values.astype(jnp.bfloat16)).astype(jnp.float32)


def reference(tokens, expert_ids, combine_weight, slot_of_expert, w_gate, w_up, w_down):
    rows = tokens.astype(jnp.float32)
    count = rows.shape[0]
    group = FF // N_DP
    slots = slot_of_expert[expert_ids]

    def add_slot(index, total):
        gate = jnp.dot(rows, w_gate[index].astype(jnp.float32), precision=lax.Precision.HIGHEST)
        upper = jnp.dot(rows, w_up[index].astype(jnp.float32), precision=lax.Precision.HIGHEST)
        hidden = round_trip(jax.nn.silu(gate) * upper)
        down = w_down[index].astype(jnp.float32).reshape(N_DP, group, D)
        parts = jnp.einsum("tqf,qfd->tqd", hidden.reshape(count, N_DP, group), down, precision=lax.Precision.HIGHEST)
        expert_out = round_trip(jnp.sum(round_trip(parts), axis=1))
        weight = jnp.sum(jnp.where(slots == index, combine_weight, jnp.float32(0.0)), axis=1)
        return total + weight[:, None] * expert_out

    total = lax.fori_loop(0, EXPERTS, add_slot, jnp.zeros((count, D), jnp.float32))
    return total.astype(jnp.bfloat16)
```

```python
import functools

import jax
import jax.numpy as jnp
from jax import lax
from jax.experimental import pallas as pl
from jax.experimental.pallas import tpu as pltpu
from jax.sharding import PartitionSpec as P

LANES = 128
PACK = 16
SOURCES = 16
HALVES = 2
MESH = pl.DeviceIdType.MESH


def slot_weights(expert_ids, combine_weight, slot_of_expert):
    experts = slot_of_expert.shape[0]
    numbers = jnp.arange(experts, dtype=jnp.int32)
    chosen = expert_ids[:, :, None] == numbers
    picked = jnp.sum(jnp.where(chosen, slot_of_expert, 0), axis=2)
    return jnp.sum(
        jnp.where(picked[:, :, None] == numbers, combine_weight[:, :, None], 0.0), axis=1
    )


def order(rows, transposed):
    side = SOURCES * PACK
    bits = rows.bit_length() - 1
    long = lax.broadcasted_iota(jnp.int32, (side, side), 1 if transposed else 0)
    short = lax.broadcasted_iota(jnp.int32, (side, side), 0 if transposed else 1)
    token = long & (rows - 1)
    device = (long >> bits) & (SOURCES - 1)
    piece = long >> (bits + SOURCES.bit_length() - 1)
    return jnp.where(short == device * PACK + piece * rows + token, 1.0, 0.0).astype(jnp.bfloat16)


def kernel(n, n_dp, rows, x_ref, wg_ref, wu_ref, wd_ref, o_ref,
           xbuf, xs, comb, wg, wu, wd, hid, ybuf, sbuf, rbuf,
           g_sem, u_sem, d_sem, xs_sem, xr_sem, rs_sem, rr_sem):
    slots = wg_ref.shape[0]
    pieces = PACK // rows
    sets = wg.shape[0]
    ring = wd.shape[0]
    span = wg.shape[2]
    half = wd.shape[2]
    part = half // pieces
    block = SOURCES * rows
    ep = lax.axis_index("ep")
    dp = lax.axis_index("dp")
    me = ep * n_dp + dp

    def gate_copies(s, place, c):
        source = (s, pl.ds(c * span, span))
        return (
            pltpu.make_async_copy(wg_ref.at[source], wg.at[place, c], g_sem.at[place, c]),
            pltpu.make_async_copy(wu_ref.at[source], wu.at[place, c], u_sem.at[place, c]),
        )

    def down_copy(i):
        return pltpu.make_async_copy(
            wd_ref.at[i % slots, :, pl.ds((i // slots) * half, half)], wd.at[i % ring], d_sem.at[i % ring]
        )

    def partner(d):
        p = lax.rem(me + d, n)
        return p, {"ep": lax.div(p, n_dp), "dp": lax.rem(p, n_dp)}

    barrier = pltpu.get_barrier_semaphore()

    def greet(d, _):
        pl.semaphore_signal(barrier, inc=1, device_id=partner(d)[1], device_id_type=MESH)
        return 0

    lax.fori_loop(1, n, greet, 0)
    for s in range(sets):
        for c in range(pieces):
            for copy in gate_copies(s, s, c):
                copy.start()
    for i in range(ring):
        down_copy(i).start()
    pl.semaphore_wait(barrier, n - 1)

    def x_copy(d):
        p, where = partner(d)
        return pltpu.make_async_remote_copy(
            src_ref=x_ref, dst_ref=xbuf.at[me], send_sem=xs_sem.at[p], recv_sem=xr_sem.at[me],
            device_id=where, device_id_type=MESH,
        )

    def x_arrival(d):
        p, where = partner(d)
        return pltpu.make_async_remote_copy(
            src_ref=x_ref, dst_ref=xbuf.at[p], send_sem=xs_sem.at[p], recv_sem=xr_sem.at[p],
            device_id=where, device_id_type=MESH,
        )

    def x_send(d, _):
        x_copy(d).start()
        return 0

    lax.fori_loop(1, n, x_send, 0)
    xbuf[me] = x_ref[...]

    def x_wait(d, _):
        x_arrival(d).wait_recv()
        return 0

    lax.fori_loop(1, n, x_wait, 0)

    forward = order(rows, False)

    def unpack(b, _):
        packed = xbuf[pl.ds(b * SOURCES, SOURCES)].reshape(SOURCES * PACK, span + LANES)
        here = pl.ds(pl.multiple_of(b * block, block), block)
        plain = jnp.dot(forward, packed, preferred_element_type=jnp.float32)
        total = plain[:block, span:]
        for c in range(1, pieces):
            total = total + plain[c * block:(c + 1) * block, span:]
        comb[here] = total
        for c in range(pieces):
            xs[c, here] = plain[c * block:(c + 1) * block, :span].astype(jnp.bfloat16)
        return 0

    lax.fori_loop(0, n // SOURCES, unpack, 0)

    def slot_step(s, _):
        place = lax.rem(s, sets)
        gate = upper = None
        for c in range(pieces):
            for copy in gate_copies(s, place, c):
                copy.wait()
            g = jnp.dot(xs[c], wg[place, c], preferred_element_type=jnp.float32)
            u = jnp.dot(xs[c], wu[place, c], preferred_element_type=jnp.float32)
            gate = g if c == 0 else gate + g
            upper = u if c == 0 else upper + u

            @pl.when(s + sets < slots)
            def _():
                for copy in gate_copies(s + sets, place, c):
                    copy.start()

        table = comb[...]
        lane = lax.broadcasted_iota(jnp.int32, table.shape, 1)
        scale = jnp.sum(jnp.where(lane == ep * slots + s, table, 0.0), axis=1, keepdims=True)
        hidden = gate / (1.0 + jnp.exp(-gate)) * upper
        hid[s] = (hidden * scale).astype(jnp.bfloat16)
        return 0

    lax.fori_loop(0, slots, slot_step, 0)

    back = order(rows, True)

    def r_copy(h, d):
        p, where = partner(d)
        return pltpu.make_async_remote_copy(
            src_ref=sbuf.at[h, p], dst_ref=rbuf.at[h, me], send_sem=rs_sem.at[h, p],
            recv_sem=rr_sem.at[h, me], device_id=where, device_id_type=MESH,
        )

    def r_arrival(h, d):
        p, where = partner(d)
        return pltpu.make_async_remote_copy(
            src_ref=sbuf.at[h, p], dst_ref=rbuf.at[h, p], send_sem=rs_sem.at[h, p],
            recv_sem=rr_sem.at[h, p], device_id=where, device_id_type=MESH,
        )

    for h in range(HALVES):
        for s in range(slots):
            down_copy(h * slots + s).wait()
        for c in range(pieces):
            columns = slice(c * part, (c + 1) * part)
            total = None
            for s in range(slots):
                y = jnp.dot(hid[s], wd[(h * slots + s) % ring, :, columns],
                            preferred_element_type=jnp.float32)
                total = y if s == 0 else total + y
            ybuf[:, c] = total.astype(jnp.bfloat16).reshape(n // SOURCES, block, part)
        for s in range(slots):
            later = h * slots + s + ring
            if later < HALVES * slots:
                down_copy(later).start()

        def pack(b, _):
            plain = ybuf[b].reshape(pieces * block, part)
            packed = jnp.dot(back, plain, preferred_element_type=jnp.float32)
            sbuf[h, pl.ds(b * SOURCES, SOURCES)] = packed.astype(jnp.bfloat16).reshape(
                SOURCES, PACK, part)
            return 0

        lax.fori_loop(0, n // SOURCES, pack, 0)

        def r_send(d, _):
            r_copy(h, d).start()
            return 0

        lax.fori_loop(1, n, r_send, 0)
        rbuf[h, me] = sbuf[h, me]

    def x_sent(d, _):
        x_copy(d).wait_send()
        return 0

    lax.fori_loop(1, n, x_sent, 0)
    for h in range(HALVES):
        def r_wait(d, _):
            r_arrival(h, d).wait_recv()
            return 0

        lax.fori_loop(1, n, r_wait, 0)

        def add(i, total):
            return total + rbuf[h, i].astype(jnp.float32)

        total = lax.fori_loop(0, n, add, jnp.zeros((PACK, part), jnp.float32))
        o_ref[h] = total.astype(jnp.bfloat16)

        def r_sent(d, _):
            r_copy(h, d).wait_send()
            return 0

        lax.fori_loop(1, n, r_sent, 0)


def body(tokens, expert_ids, combine_weight, slot_of_expert, w_gate, w_up, w_down):
    n_dp = lax.axis_size("dp")
    n = lax.axis_size("ep") * n_dp
    rows, width = tokens.shape
    slots, _, units = w_gate.shape
    pieces = PACK // rows
    span = width // pieces
    half = width // HALVES
    part = half // pieces
    sets = min(2, slots)
    ring = min(6, HALVES * slots)
    table = slot_weights(expert_ids, combine_weight, slot_of_expert)
    high = lax.reduce_precision(table, 8, 7)
    middle = lax.reduce_precision(table - high, 8, 7)
    low = table - high - middle
    extra = jnp.stack([high, middle, low] + [jnp.zeros_like(low)] * (pieces - 3))
    extra = jnp.pad(extra, ((0, 0), (0, 0), (0, LANES - extra.shape[2])))
    packed = jnp.concatenate([
        jnp.transpose(tokens.reshape(rows, pieces, span), (1, 0, 2)).reshape(PACK, span),
        extra.reshape(PACK, LANES).astype(jnp.bfloat16),
    ], axis=1)
    vmem = pl.BlockSpec(memory_space=pltpu.VMEM)
    hbm = pl.BlockSpec(memory_space=pl.ANY)
    bf16 = jnp.bfloat16
    dma = pltpu.SemaphoreType.DMA
    out = pl.pallas_call(
        functools.partial(kernel, n, n_dp, rows),
        out_shape=jax.ShapeDtypeStruct((HALVES, PACK, part), bf16),
        in_specs=[vmem, hbm, hbm, hbm],
        out_specs=vmem,
        scratch_shapes=[
            pltpu.VMEM((n, PACK, span + LANES), bf16),
            pltpu.VMEM((pieces, n * rows, span), bf16),
            pltpu.VMEM((n * rows, LANES), jnp.float32),
            pltpu.VMEM((sets, pieces, span, units), bf16),
            pltpu.VMEM((sets, pieces, span, units), bf16),
            pltpu.VMEM((ring, units, half), bf16),
            pltpu.VMEM((slots, n * rows, units), bf16),
            pltpu.VMEM((n // SOURCES, pieces, SOURCES * rows, part), bf16),
            pltpu.VMEM((HALVES, n, PACK, part), bf16),
            pltpu.VMEM((HALVES, n, PACK, part), bf16),
            dma((sets, pieces)),
            dma((sets, pieces)),
            dma((ring,)),
            dma((n,)),
            dma((n,)),
            dma((HALVES, n)),
            dma((HALVES, n)),
        ],
        compiler_params=pltpu.CompilerParams(
            collective_id=0, has_side_effects=True, vmem_limit_bytes=60 * 2**20
        ),
        cost_estimate=pl.CostEstimate(
            flops=6 * n * rows * slots * width * units,
            bytes_accessed=6 * slots * width * units,
            transcendentals=n * rows * slots * units,
        ),
    )(packed, w_gate, w_up, w_down)
    out = out.reshape(HALVES, pieces, rows, part)
    return jnp.transpose(out, (2, 0, 1, 3)).reshape(rows, width)


def solution(mesh):
    in_specs = (
        P(("grp", "ep", "dp"), None),
        P(("grp", "ep", "dp"), None),
        P(("grp", "ep", "dp"), None),
        P(),
        P("ep", None, "dp"),
        P("ep", None, "dp"),
        P("ep", "dp", None),
    )
    out_specs = P(("grp", "ep", "dp"), None)
    return jax.shard_map(body, mesh=mesh, in_specs=in_specs, out_specs=out_specs, check_vma=False)
```

```python
import functools

import jax
import jax.numpy as jnp
from jax import lax
from jax.experimental import pallas as pl
from jax.experimental.pallas import tpu as pltpu
from jax.sharding import PartitionSpec as P

LANES = 128
PACK = 16
SOURCES = 16
HALVES = 2
MESH = pl.DeviceIdType.MESH


def slot_weights(ids, weights, slot_ref):
    shape = (ids.shape[0], LANES)
    lane = lax.broadcasted_iota(jnp.int32, shape, 1)
    by_expert = jnp.zeros(shape, jnp.float32)
    for k in range(ids.shape[1]):
        by_expert += jnp.where(lane == ids[:, k:k + 1], weights[:, k:k + 1], 0.0)
    by_slot = jnp.zeros(shape, jnp.float32)
    for e in range(slot_ref.shape[0]):
        by_slot += jnp.where(lane == slot_ref[e], by_expert[:, e:e + 1], 0.0)
    return by_slot


def order(rows, transposed):
    side = SOURCES * PACK
    bits = rows.bit_length() - 1
    long = lax.broadcasted_iota(jnp.int32, (side, side), 1 if transposed else 0)
    short = lax.broadcasted_iota(jnp.int32, (side, side), 0 if transposed else 1)
    token = long & (rows - 1)
    device = (long >> bits) & (SOURCES - 1)
    piece = long >> (bits + SOURCES.bit_length() - 1)
    if transposed:
        device = (device & 1) * (SOURCES // 2) + (device >> 1)
    return jnp.where(short == device * PACK + piece * rows + token, 1.0, 0.0).astype(jnp.bfloat16)


def kernel(n, n_dp, rows, t_ref, id_ref, cw_ref, so_ref, wg_ref, wu_ref, wd_ref, o_ref,
           xp, xbuf, xs, comb, wg, wu, wd, hid, ybuf, sbuf, pbuf, tbuf, rbuf,
           g_sem, u_sem, d_sem, xs_sem, xr_sem, fs_sem, ps_sem, pr_sem, rs_sem, rr_sem):
    slots = wg_ref.shape[0]
    pieces = PACK // rows
    sets = wg.shape[0]
    ring = wd.shape[0]
    span = wg.shape[2]
    half = wd.shape[2]
    part = half // pieces
    block = SOURCES * rows
    ep = lax.axis_index("ep")
    dp = lax.axis_index("dp")
    me = ep * n_dp + dp
    chips = n // 2
    chip, core = lax.div(me, 2), lax.rem(me, 2)
    other = 1 - core

    def gate_copies(s, place, c):
        source = (s, pl.ds(c * span, span))
        return (
            pltpu.make_async_copy(wg_ref.at[source], wg.at[place, c], g_sem.at[place, c]),
            pltpu.make_async_copy(wu_ref.at[source], wu.at[place, c], u_sem.at[place, c]),
        )

    def down_copy(i):
        return pltpu.make_async_copy(
            wd_ref.at[i % slots, :, pl.ds((i // slots) * half, half)], wd.at[i % ring], d_sem.at[i % ring]
        )

    def place_of(p):
        return {"ep": lax.div(p, n_dp), "dp": lax.rem(p, n_dp)}

    sibling = place_of(2 * chip + other)

    def ahead(d):
        return lax.rem(chip + d, chips)

    def behind(d):
        return lax.rem(chip + chips - d, chips)

    barrier = pltpu.get_barrier_semaphore()

    def greet(d, _):
        pl.semaphore_signal(
            barrier, inc=1, device_id=place_of(2 * ahead(d) + core), device_id_type=MESH)
        return 0

    pl.semaphore_signal(barrier, inc=1, device_id=sibling, device_id_type=MESH)
    lax.fori_loop(1, chips, greet, 0)
    for s in range(sets):
        for c in range(pieces):
            for copy in gate_copies(s, s, c):
                copy.start()
    for i in range(ring):
        down_copy(i).start()
    table = slot_weights(id_ref[...], cw_ref[...], so_ref)
    high = table.astype(jnp.bfloat16).astype(jnp.float32)
    middle = (table - high).astype(jnp.bfloat16).astype(jnp.float32)
    terms = [high, middle, table - high - middle] + [jnp.zeros_like(table)] * (pieces - 3)
    xp[:, :span] = jnp.concatenate(
        [t_ref[:, c * span:(c + 1) * span].astype(jnp.float32) for c in range(pieces)], axis=0
    ).astype(jnp.bfloat16)
    xp[:, span:] = jnp.concatenate(terms, axis=0).astype(jnp.bfloat16)
    pl.semaphore_wait(barrier, chips)

    def x_copy(source, target, to_chip, to_core, landed, sent):
        return pltpu.make_async_remote_copy(
            src_ref=source, dst_ref=xbuf.at[target], send_sem=sent, recv_sem=xr_sem.at[landed],
            device_id=place_of(2 * to_chip + to_core), device_id_type=MESH,
        )

    def x_send(d, _):
        x_copy(xp, me, ahead(d), core, me, xs_sem.at[ahead(d)]).start()
        return 0

    def x_pass(d, _):
        p = 2 * behind(d) + core
        x_copy(xp, p, behind(d), core, p, xs_sem.at[behind(d)]).wait_recv()
        x_copy(xbuf.at[p], p, chip, other, p, fs_sem.at[behind(d)]).start()
        return 0

    def x_wait(d, _):
        p = 2 * behind(d) + other
        x_copy(xp, p, chip, other, p, fs_sem.at[behind(d)]).wait_recv()
        return 0

    lax.fori_loop(1, chips, x_send, 0)
    x_copy(xp, me, chip, other, me, fs_sem.at[chip]).start()
    xbuf[me] = xp[...]
    lax.fori_loop(1, chips, x_pass, 0)
    lax.fori_loop(0, chips, x_wait, 0)

    forward = order(rows, False)

    def unpack(b, _):
        packed = xbuf[pl.ds(b * SOURCES, SOURCES)].reshape(SOURCES * PACK, span + LANES)
        here = pl.ds(pl.multiple_of(b * block, block), block)
        plain = jnp.dot(forward, packed, preferred_element_type=jnp.float32)
        total = plain[:block, span:]
        for c in range(1, pieces):
            total = total + plain[c * block:(c + 1) * block, span:]
        comb[here] = total
        for c in range(pieces):
            xs[c, here] = plain[c * block:(c + 1) * block, :span].astype(jnp.bfloat16)
        return 0

    lax.fori_loop(0, n // SOURCES, unpack, 0)

    def slot_step(s, _):
        place = lax.rem(s, sets)
        gate = upper = None
        for c in range(pieces):
            for copy in gate_copies(s, place, c):
                copy.wait()
            g = jnp.dot(xs[c], wg[place, c], preferred_element_type=jnp.float32)
            u = jnp.dot(xs[c], wu[place, c], preferred_element_type=jnp.float32)
            gate = g if c == 0 else gate + g
            upper = u if c == 0 else upper + u

            @pl.when(s + sets < slots)
            def _():
                for copy in gate_copies(s + sets, place, c):
                    copy.start()

        table = comb[...]
        lane = lax.broadcasted_iota(jnp.int32, table.shape, 1)
        scale = jnp.sum(jnp.where(lane == ep * slots + s, table, 0.0), axis=1, keepdims=True)
        hidden = gate / (1.0 + jnp.exp(-gate)) * upper
        hid[s] = (hidden * scale).astype(jnp.bfloat16)
        return 0

    lax.fori_loop(0, slots, slot_step, 0)

    back = order(rows, True)

    def pair_copy(h):
        return pltpu.make_async_remote_copy(
            src_ref=sbuf.at[h, other], dst_ref=pbuf.at[h], send_sem=ps_sem.at[h],
            recv_sem=pr_sem.at[h], device_id=sibling, device_id_type=MESH,
        )

    def r_copy(h, to, landed):
        return pltpu.make_async_remote_copy(
            src_ref=tbuf.at[h, to], dst_ref=rbuf.at[h, landed], send_sem=rs_sem.at[h, to],
            recv_sem=rr_sem.at[h, landed], device_id=place_of(2 * to + core), device_id_type=MESH,
        )

    def reduce_pair(h):
        pair_copy(h).wait()

        def r_send(d, _):
            to = ahead(d)
            both = sbuf[h, core, to].astype(jnp.float32) + pbuf[h, to].astype(jnp.float32)
            tbuf[h, to] = both.astype(jnp.bfloat16)
            r_copy(h, to, chip).start()
            return 0

        lax.fori_loop(1, chips, r_send, 0)

    for h in range(HALVES):
        for s in range(slots):
            down_copy(h * slots + s).wait()
        for c in range(pieces):
            columns = slice(c * part, (c + 1) * part)
            total = None
            for s in range(slots):
                y = jnp.dot(hid[s], wd[(h * slots + s) % ring, :, columns],
                            preferred_element_type=jnp.float32)
                total = y if s == 0 else total + y
            if h > 0 and c == 0:
                reduce_pair(h - 1)
            ybuf[:, c] = total.astype(jnp.bfloat16).reshape(n // SOURCES, block, part)
        for s in range(slots):
            later = h * slots + s + ring
            if later < HALVES * slots:
                down_copy(later).start()

        def pack(b, _):
            plain = ybuf[b].reshape(pieces * block, part)
            packed = jnp.dot(back, plain, preferred_element_type=jnp.float32)
            packed = packed.astype(jnp.bfloat16).reshape(2, SOURCES // 2, PACK, part)
            sbuf[h, :, pl.ds(b * (SOURCES // 2), SOURCES // 2)] = packed
            return 0

        lax.fori_loop(0, n // SOURCES, pack, 0)
        pair_copy(h).start()
    reduce_pair(HALVES - 1)

    def x_sent(d, _):
        x_copy(xp, me, ahead(d), core, me, xs_sem.at[ahead(d)]).wait_send()
        return 0

    def x_passed(d, _):
        x_copy(xp, me, chip, other, me, fs_sem.at[behind(d)]).wait_send()
        return 0

    lax.fori_loop(1, chips, x_sent, 0)
    lax.fori_loop(0, chips, x_passed, 0)
    for h in range(HALVES):
        total = sbuf[h, core, chip].astype(jnp.float32) + pbuf[h, chip].astype(jnp.float32)

        def add(d, total):
            r_copy(h, behind(d), behind(d)).wait_recv()
            return total + rbuf[h, behind(d)].astype(jnp.float32)

        total = lax.fori_loop(1, chips, add, total)
        for c in range(pieces):
            o_ref[:, h * half + c * part:h * half + (c + 1) * part] = (
                total[c * rows:(c + 1) * rows].astype(jnp.bfloat16))

        def r_sent(d, _):
            r_copy(h, ahead(d), chip).wait_send()
            return 0

        lax.fori_loop(1, chips, r_sent, 0)


def body(tokens, expert_ids, combine_weight, slot_of_expert, w_gate, w_up, w_down):
    n_dp = lax.axis_size("dp")
    n = lax.axis_size("ep") * n_dp
    rows, width = tokens.shape
    slots, _, units = w_gate.shape
    pieces = PACK // rows
    span = width // pieces
    half = width // HALVES
    part = half // pieces
    sets = min(2, slots)
    ring = min(6, HALVES * slots)
    vmem = pl.BlockSpec(memory_space=pltpu.VMEM)
    hbm = pl.BlockSpec(memory_space=pl.ANY)
    bf16 = jnp.bfloat16
    dma = pltpu.SemaphoreType.DMA
    return pl.pallas_call(
        functools.partial(kernel, n, n_dp, rows),
        out_shape=jax.ShapeDtypeStruct((rows, width), bf16),
        in_specs=[vmem, vmem, vmem, pl.BlockSpec(memory_space=pltpu.SMEM), hbm, hbm, hbm],
        out_specs=vmem,
        scratch_shapes=[
            pltpu.VMEM((PACK, span + LANES), bf16),
            pltpu.VMEM((n, PACK, span + LANES), bf16),
            pltpu.VMEM((pieces, n * rows, span), bf16),
            pltpu.VMEM((n * rows, LANES), jnp.float32),
            pltpu.VMEM((sets, pieces, span, units), bf16),
            pltpu.VMEM((sets, pieces, span, units), bf16),
            pltpu.VMEM((ring, units, half), bf16),
            pltpu.VMEM((slots, n * rows, units), bf16),
            pltpu.VMEM((n // SOURCES, pieces, SOURCES * rows, part), bf16),
            pltpu.VMEM((HALVES, 2, n // 2, PACK, part), bf16),
            pltpu.VMEM((HALVES, n // 2, PACK, part), bf16),
            pltpu.VMEM((HALVES, n // 2, PACK, part), bf16),
            pltpu.VMEM((HALVES, n // 2, PACK, part), bf16),
            dma((sets, pieces)),
            dma((sets, pieces)),
            dma((ring,)),
            dma((n // 2,)),
            dma((n,)),
            dma((n // 2,)),
            dma((HALVES,)),
            dma((HALVES,)),
            dma((HALVES, n // 2)),
            dma((HALVES, n // 2)),
        ],
        compiler_params=pltpu.CompilerParams(
            collective_id=0, has_side_effects=True, vmem_limit_bytes=60 * 2**20
        ),
        cost_estimate=pl.CostEstimate(
            flops=6 * n * rows * slots * width * units,
            bytes_accessed=6 * slots * width * units,
            transcendentals=n * rows * slots * units,
        ),
    )(tokens, expert_ids, combine_weight, slot_of_expert, w_gate, w_up, w_down)


def solution(mesh):
    in_specs = (
        P(("grp", "ep", "dp"), None),
        P(("grp", "ep", "dp"), None),
        P(("grp", "ep", "dp"), None),
        P(),
        P("ep", None, "dp"),
        P("ep", None, "dp"),
        P("ep", "dp", None),
    )
    out_specs = P(("grp", "ep", "dp"), None)
    return jax.shard_map(body, mesh=mesh, in_specs=in_specs, out_specs=out_specs, check_vma=False)
```

```python
import functools

import jax
import jax.numpy as jnp
from jax import lax
from jax.experimental import pallas as pl
from jax.experimental.pallas import tpu as pltpu
from jax.sharding import PartitionSpec as P

LANES = 128
PACK = 16
SOURCES = 16
HALVES = 2
MESH = pl.DeviceIdType.MESH


def slot_weights(ids, weights, slot_ref):
    shape = (ids.shape[0], LANES)
    lane = lax.broadcasted_iota(jnp.int32, shape, 1)
    by_expert = jnp.zeros(shape, jnp.float32)
    for k in range(ids.shape[1]):
        by_expert += jnp.where(lane == ids[:, k:k + 1], weights[:, k:k + 1], 0.0)
    by_slot = jnp.zeros(shape, jnp.float32)
    for e in range(slot_ref.shape[0]):
        by_slot += jnp.where(lane == slot_ref[e], by_expert[:, e:e + 1], 0.0)
    return by_slot


def order(rows, transposed):
    side = SOURCES * PACK
    bits = rows.bit_length() - 1
    long = lax.broadcasted_iota(jnp.int32, (side, side), 1 if transposed else 0)
    short = lax.broadcasted_iota(jnp.int32, (side, side), 0 if transposed else 1)
    token = long & (rows - 1)
    device = (long >> bits) & (SOURCES - 1)
    piece = long >> (bits + SOURCES.bit_length() - 1)
    if transposed:
        device = (device & 1) * (SOURCES // 2) + (device >> 1)
    return jnp.where(short == device * PACK + piece * rows + token, 1.0, 0.0).astype(jnp.bfloat16)


def kernel(n, n_dp, rows, t_ref, id_ref, cw_ref, so_ref, wg_ref, wu_ref, wd_ref, o_ref,
           xp0, xp1, xbuf0, xbuf1, xs, comb, gacc, uacc, wg, wu, wd, hid, ybuf, sbuf, pbuf, tbuf, rbuf,
           g_sem, u_sem, d_sem, xs_sem, xr_sem, fs_sem, ps_sem, pr_sem, rs_sem, rr_sem):
    slots = wg_ref.shape[0]
    pieces = PACK // rows
    depth = wg.shape[0]
    xp, xbuf = (xp0, xp1), (xbuf0, xbuf1)
    ring = wd.shape[0]
    half = wd.shape[2]
    part = half // pieces
    block = SOURCES * rows
    ep = lax.axis_index("ep")
    dp = lax.axis_index("dp")
    me = ep * n_dp + dp
    chips = n // 2
    chip, core = lax.div(me, 2), lax.rem(me, 2)
    other = 1 - core

    def gate_copies(step):
        place = lax.rem(step, depth)
        source = (lax.rem(step, slots), pl.ds(pl.multiple_of(lax.div(step, slots) * half, half), half))
        return (
            pltpu.make_async_copy(wg_ref.at[source], wg.at[place], g_sem.at[place]),
            pltpu.make_async_copy(wu_ref.at[source], wu.at[place], u_sem.at[place]),
        )

    def down_copy(i):
        return pltpu.make_async_copy(
            wd_ref.at[i % slots, :, pl.ds((i // slots) * half, half)], wd.at[i % ring], d_sem.at[i % ring]
        )

    def place_of(p):
        return {"ep": lax.div(p, n_dp), "dp": lax.rem(p, n_dp)}

    sibling = place_of(2 * chip + other)

    def ahead(d):
        return lax.rem(chip + d, chips)

    def behind(d):
        return lax.rem(chip + chips - d, chips)

    barrier = pltpu.get_barrier_semaphore()

    def greet(d, _):
        pl.semaphore_signal(
            barrier, inc=1, device_id=place_of(2 * ahead(d) + core), device_id_type=MESH)
        return 0

    pl.semaphore_signal(barrier, inc=1, device_id=sibling, device_id_type=MESH)
    lax.fori_loop(1, chips, greet, 0)
    for step in range(depth):
        for copy in gate_copies(jnp.int32(step)):
            copy.start()
    for i in range(ring):
        down_copy(i).start()
    table = slot_weights(id_ref[...], cw_ref[...], so_ref)
    high = table.astype(jnp.bfloat16).astype(jnp.float32)
    middle = (table - high).astype(jnp.bfloat16).astype(jnp.float32)
    terms = [high, middle, table - high - middle] + [jnp.zeros_like(table)] * (pieces - 3)
    for h in range(HALVES):
        xp[h][:, :part] = jnp.concatenate(
            [t_ref[:, h * half + c * part:h * half + (c + 1) * part].astype(jnp.float32)
             for c in range(pieces)], axis=0).astype(jnp.bfloat16)
    xp0[:, part:] = jnp.concatenate(terms, axis=0).astype(jnp.bfloat16)
    pl.semaphore_wait(barrier, chips)

    def across(h, to, landed):
        return pltpu.make_async_remote_copy(
            src_ref=xp[h], dst_ref=xbuf[h].at[landed], send_sem=xs_sem.at[h, to],
            recv_sem=xr_sem.at[h, landed], device_id=place_of(2 * to + core), device_id_type=MESH,
        )

    def within(h, source, landed):
        return pltpu.make_async_remote_copy(
            src_ref=source, dst_ref=xbuf[h].at[landed], send_sem=fs_sem.at[h, lax.div(landed, 2)],
            recv_sem=xr_sem.at[h, landed], device_id=sibling, device_id_type=MESH,
        )

    for h in range(HALVES):
        def x_send(d, _):
            across(h, ahead(d), me).start()
            return 0

        lax.fori_loop(1, chips, x_send, 0)
        within(h, xp[h], me).start()
        xbuf[h][me] = xp[h][...]

    def pass_on(h):
        def x_pass(d, _):
            p = 2 * behind(d) + core
            across(h, behind(d), p).wait_recv()
            within(h, xbuf[h].at[p], p).start()
            return 0

        lax.fori_loop(1, chips, x_pass, 0)

    forward = order(rows, False)

    def gather(h):
        def x_wait(d, _):
            within(h, xp[h], 2 * behind(d) + other).wait_recv()
            return 0

        lax.fori_loop(0, chips, x_wait, 0)

        def unpack(b, _):
            packed = xbuf[h][pl.ds(b * SOURCES, SOURCES)].reshape(SOURCES * PACK, xbuf[h].shape[2])
            here = pl.ds(pl.multiple_of(b * block, block), block)
            plain = jnp.dot(forward, packed, preferred_element_type=jnp.float32)
            if h == 0:
                total = plain[:block, part:]
                for c in range(1, pieces):
                    total = total + plain[c * block:(c + 1) * block, part:]
                comb[here] = total
            for c in range(pieces):
                xs[h, here, c * part:(c + 1) * part] = (
                    plain[c * block:(c + 1) * block, :part].astype(jnp.bfloat16))
            return 0

        lax.fori_loop(0, n // SOURCES, unpack, 0)

    def slot_step(h, s):
        step = h * slots + s
        place = lax.rem(step, depth)
        for copy in gate_copies(step):
            copy.wait()
        gate = jnp.dot(xs[h], wg[place], preferred_element_type=jnp.float32)
        upper = jnp.dot(xs[h], wu[place], preferred_element_type=jnp.float32)

        @pl.when(step + depth < HALVES * slots)
        def _():
            for copy in gate_copies(step + depth):
                copy.start()

        if h == 0:
            gacc[s] = gate
            uacc[s] = upper
            return 0
        gate = gate + gacc[s]
        upper = upper + uacc[s]
        table = comb[...]
        lane = lax.broadcasted_iota(jnp.int32, table.shape, 1)
        scale = jnp.sum(jnp.where(lane == ep * slots + s, table, 0.0), axis=1, keepdims=True)
        hidden = gate / (1.0 + jnp.exp(-gate)) * upper
        hid[s] = (hidden * scale).astype(jnp.bfloat16)
        return 0

    middle_slot = slots // 2
    pass_on(0)
    gather(0)
    lax.fori_loop(0, middle_slot, lambda s, _: slot_step(0, s), 0)
    pass_on(1)
    lax.fori_loop(middle_slot, slots, lambda s, _: slot_step(0, s), 0)
    gather(1)
    lax.fori_loop(0, slots, lambda s, _: slot_step(1, s), 0)

    back = order(rows, True)

    def pair_copy(h):
        return pltpu.make_async_remote_copy(
            src_ref=sbuf.at[h, other], dst_ref=pbuf.at[h], send_sem=ps_sem.at[h],
            recv_sem=pr_sem.at[h], device_id=sibling, device_id_type=MESH,
        )

    def r_copy(h, to, landed):
        return pltpu.make_async_remote_copy(
            src_ref=tbuf.at[h, to], dst_ref=rbuf.at[h, landed], send_sem=rs_sem.at[h, to],
            recv_sem=rr_sem.at[h, landed], device_id=place_of(2 * to + core), device_id_type=MESH,
        )

    def reduce_pair(h):
        pair_copy(h).wait()

        def r_send(d, _):
            to = ahead(d)
            both = sbuf[h, core, to].astype(jnp.float32) + pbuf[h, to].astype(jnp.float32)
            tbuf[h, to] = both.astype(jnp.bfloat16)
            r_copy(h, to, chip).start()
            return 0

        lax.fori_loop(1, chips, r_send, 0)

    for h in range(HALVES):
        for c in range(pieces):
            columns = slice(c * part, (c + 1) * part)
            total = None
            for s in range(slots):
                if c == 0:
                    down_copy(h * slots + s).wait()
                y = jnp.dot(hid[s], wd[(h * slots + s) % ring, :, columns],
                            preferred_element_type=jnp.float32)
                total = y if s == 0 else total + y
                later = h * slots + s + ring
                if c == pieces - 1 and later < HALVES * slots:
                    down_copy(later).start()
            if h > 0 and c == 0:
                reduce_pair(h - 1)
            ybuf[:, c] = total.astype(jnp.bfloat16).reshape(n // SOURCES, block, part)

        def pack(b, _):
            plain = ybuf[b].reshape(pieces * block, part)
            packed = jnp.dot(back, plain, preferred_element_type=jnp.float32)
            packed = packed.astype(jnp.bfloat16).reshape(2, SOURCES // 2, PACK, part)
            sbuf[h, :, pl.ds(b * (SOURCES // 2), SOURCES // 2)] = packed
            return 0

        lax.fori_loop(0, n // SOURCES, pack, 0)
        pair_copy(h).start()
    reduce_pair(HALVES - 1)

    for h in range(HALVES):
        def x_sent(d, _):
            across(h, ahead(d), me).wait_send()
            return 0

        def x_passed(d, _):
            within(h, xp[h], 2 * behind(d) + core).wait_send()
            return 0

        lax.fori_loop(1, chips, x_sent, 0)
        lax.fori_loop(0, chips, x_passed, 0)
    for h in range(HALVES):
        total = sbuf[h, core, chip].astype(jnp.float32) + pbuf[h, chip].astype(jnp.float32)

        def add(d, total):
            r_copy(h, behind(d), behind(d)).wait_recv()
            return total + rbuf[h, behind(d)].astype(jnp.float32)

        total = lax.fori_loop(1, chips, add, total)
        for c in range(pieces):
            o_ref[:, h * half + c * part:h * half + (c + 1) * part] = (
                total[c * rows:(c + 1) * rows].astype(jnp.bfloat16))

        def r_sent(d, _):
            r_copy(h, ahead(d), chip).wait_send()
            return 0

        lax.fori_loop(1, chips, r_sent, 0)


def body(tokens, expert_ids, combine_weight, slot_of_expert, w_gate, w_up, w_down):
    n_dp = lax.axis_size("dp")
    n = lax.axis_size("ep") * n_dp
    rows, width = tokens.shape
    slots, _, units = w_gate.shape
    pieces = PACK // rows
    half = width // HALVES
    part = half // pieces
    depth = min(4, HALVES * slots)
    ring = min(5, HALVES * slots)
    vmem = pl.BlockSpec(memory_space=pltpu.VMEM)
    hbm = pl.BlockSpec(memory_space=pl.ANY)
    bf16 = jnp.bfloat16
    dma = pltpu.SemaphoreType.DMA
    return pl.pallas_call(
        functools.partial(kernel, n, n_dp, rows),
        out_shape=jax.ShapeDtypeStruct((rows, width), bf16),
        in_specs=[vmem, vmem, vmem, pl.BlockSpec(memory_space=pltpu.SMEM), hbm, hbm, hbm],
        out_specs=vmem,
        scratch_shapes=[
            pltpu.VMEM((PACK, part + LANES), bf16),
            pltpu.VMEM((PACK, part), bf16),
            pltpu.VMEM((n, PACK, part + LANES), bf16),
            pltpu.VMEM((n, PACK, part), bf16),
            pltpu.VMEM((HALVES, n * rows, half), bf16),
            pltpu.VMEM((n * rows, LANES), jnp.float32),
            pltpu.VMEM((slots, n * rows, units), jnp.float32),
            pltpu.VMEM((slots, n * rows, units), jnp.float32),
            pltpu.VMEM((depth, half, units), bf16),
            pltpu.VMEM((depth, half, units), bf16),
            pltpu.VMEM((ring, units, half), bf16),
            pltpu.VMEM((slots, n * rows, units), bf16),
            pltpu.VMEM((n // SOURCES, pieces, SOURCES * rows, part), bf16),
            pltpu.VMEM((HALVES, 2, n // 2, PACK, part), bf16),
            pltpu.VMEM((HALVES, n // 2, PACK, part), bf16),
            pltpu.VMEM((HALVES, n // 2, PACK, part), bf16),
            pltpu.VMEM((HALVES, n // 2, PACK, part), bf16),
            dma((depth,)),
            dma((depth,)),
            dma((ring,)),
            dma((HALVES, n // 2)),
            dma((HALVES, n)),
            dma((HALVES, n // 2)),
            dma((HALVES,)),
            dma((HALVES,)),
            dma((HALVES, n // 2)),
            dma((HALVES, n // 2)),
        ],
        compiler_params=pltpu.CompilerParams(
            collective_id=0, has_side_effects=True, vmem_limit_bytes=60 * 2**20
        ),
        cost_estimate=pl.CostEstimate(
            flops=6 * n * rows * slots * width * units,
            bytes_accessed=6 * slots * width * units,
            transcendentals=n * rows * slots * units,
        ),
    )(tokens, expert_ids, combine_weight, slot_of_expert, w_gate, w_up, w_down)


def solution(mesh):
    in_specs = (
        P(("grp", "ep", "dp"), None),
        P(("grp", "ep", "dp"), None),
        P(("grp", "ep", "dp"), None),
        P(),
        P("ep", None, "dp"),
        P("ep", None, "dp"),
        P("ep", "dp", None),
    )
    out_specs = P(("grp", "ep", "dp"), None)
    return jax.shard_map(body, mesh=mesh, in_specs=in_specs, out_specs=out_specs, check_vma=False)
```

```python
import functools

import jax
import jax.numpy as jnp
from jax import lax
from jax.experimental import pallas as pl
from jax.experimental.pallas import tpu as pltpu
from jax.sharding import PartitionSpec as P

LANES = 128
PACK = 16
SOURCES = 16
HALVES = 2
MESH = pl.DeviceIdType.MESH


def slot_weights(ids, weights, slot_ref):
    shape = (ids.shape[0], LANES)
    lane = lax.broadcasted_iota(jnp.int32, shape, 1)
    by_expert = jnp.zeros(shape, jnp.float32)
    for k in range(ids.shape[1]):
        by_expert += jnp.where(lane == ids[:, k:k + 1], weights[:, k:k + 1], 0.0)
    by_slot = jnp.zeros(shape, jnp.float32)
    for e in range(slot_ref.shape[0]):
        by_slot += jnp.where(lane == slot_ref[e], by_expert[:, e:e + 1], 0.0)
    return by_slot


def order(rows, transposed):
    side = SOURCES * PACK
    bits = rows.bit_length() - 1
    long = lax.broadcasted_iota(jnp.int32, (side, side), 1 if transposed else 0)
    short = lax.broadcasted_iota(jnp.int32, (side, side), 0 if transposed else 1)
    token = long & (rows - 1)
    device = (long >> bits) & (SOURCES - 1)
    piece = long >> (bits + SOURCES.bit_length() - 1)
    if transposed:
        device = (device & 1) * (SOURCES // 2) + (device >> 1)
    return jnp.where(short == device * PACK + piece * rows + token, 1.0, 0.0).astype(jnp.bfloat16)


def kernel(n, n_dp, rows, t_ref, id_ref, cw_ref, so_ref, wg_ref, wu_ref, wd_ref, o_ref,
           xp0, xp1, xbuf0, xbuf1, xs, comb, gacc, uacc, wg, wu, wd, hid, ybuf, sbuf, pbuf, tbuf, rbuf,
           g_sem, u_sem, d_sem, xs_sem, xr_sem, fs_sem, ps_sem, pr_sem, rs_sem, rr_sem):
    slots = wg_ref.shape[0]
    pieces = PACK // rows
    depth = wg.shape[0]
    xp, xbuf = (xp0, xp1), (xbuf0, xbuf1)
    ring = wd.shape[0]
    half = wd.shape[2]
    part = half // pieces
    block = SOURCES * rows
    ep = lax.axis_index("ep")
    dp = lax.axis_index("dp")
    me = ep * n_dp + dp
    chips = n // 2
    chip, core = lax.div(me, 2), lax.rem(me, 2)
    other = 1 - core

    def gate_copies(step):
        place = lax.rem(step, depth)
        source = (lax.rem(step, slots), pl.ds(pl.multiple_of(lax.div(step, slots) * half, half), half))
        return (
            pltpu.make_async_copy(wg_ref.at[source], wg.at[place], g_sem.at[place]),
            pltpu.make_async_copy(wu_ref.at[source], wu.at[place], u_sem.at[place]),
        )

    def down_copy(i):
        return pltpu.make_async_copy(
            wd_ref.at[i % slots, :, pl.ds((i // slots) * half, half)], wd.at[i % ring], d_sem.at[i % ring]
        )

    def place_of(p):
        return {"ep": lax.div(p, n_dp), "dp": lax.rem(p, n_dp)}

    sibling = place_of(2 * chip + other)

    def ahead(d):
        return lax.rem(chip + d, chips)

    def behind(d):
        return lax.rem(chip + chips - d, chips)

    barrier = pltpu.get_barrier_semaphore()

    def greet(d, _):
        pl.semaphore_signal(
            barrier, inc=1, device_id=place_of(2 * ahead(d) + core), device_id_type=MESH)
        return 0

    pl.semaphore_signal(barrier, inc=1, device_id=sibling, device_id_type=MESH)
    lax.fori_loop(1, chips, greet, 0)
    for step in range(depth):
        for copy in gate_copies(jnp.int32(step)):
            copy.start()
    table = slot_weights(id_ref[...], cw_ref[...], so_ref)
    high = table.astype(jnp.bfloat16).astype(jnp.float32)
    middle = (table - high).astype(jnp.bfloat16).astype(jnp.float32)
    terms = [high, middle, table - high - middle] + [jnp.zeros_like(table)] * (pieces - 3)
    for h in range(HALVES):
        xp[h][:, :part] = jnp.concatenate(
            [t_ref[:, h * half + c * part:h * half + (c + 1) * part].astype(jnp.float32)
             for c in range(pieces)], axis=0).astype(jnp.bfloat16)
    xp0[:, part:] = jnp.concatenate(terms, axis=0).astype(jnp.bfloat16)
    pl.semaphore_wait(barrier, chips)

    def across(h, to, landed):
        return pltpu.make_async_remote_copy(
            src_ref=xp[h], dst_ref=xbuf[h].at[landed], send_sem=xs_sem.at[h, to],
            recv_sem=xr_sem.at[h, landed], device_id=place_of(2 * to + core), device_id_type=MESH,
        )

    def within(h, source, landed):
        return pltpu.make_async_remote_copy(
            src_ref=source, dst_ref=xbuf[h].at[landed], send_sem=fs_sem.at[h, lax.div(landed, 2)],
            recv_sem=xr_sem.at[h, landed], device_id=sibling, device_id_type=MESH,
        )

    for h in range(HALVES):
        def x_send(d, _):
            across(h, ahead(d), me).start()
            return 0

        lax.fori_loop(1, chips, x_send, 0)
        within(h, xp[h], me).start()
        xbuf[h][me] = xp[h][...]

    def pass_on(h):
        def x_pass(d, _):
            p = 2 * behind(d) + core
            across(h, behind(d), p).wait_recv()
            within(h, xbuf[h].at[p], p).start()
            return 0

        lax.fori_loop(1, chips, x_pass, 0)

    forward = order(rows, False)

    def gather(h):
        def x_wait(d, _):
            within(h, xp[h], 2 * behind(d) + other).wait_recv()
            return 0

        lax.fori_loop(0, chips, x_wait, 0)

        def unpack(b, _):
            packed = xbuf[h][pl.ds(b * SOURCES, SOURCES)].reshape(SOURCES * PACK, xbuf[h].shape[2])
            here = pl.ds(pl.multiple_of(b * block, block), block)
            plain = jnp.dot(forward, packed, preferred_element_type=jnp.float32)
            if h == 0:
                total = plain[:block, part:]
                for c in range(1, pieces):
                    total = total + plain[c * block:(c + 1) * block, part:]
                comb[here] = total
            for c in range(pieces):
                xs[h, here, c * part:(c + 1) * part] = (
                    plain[c * block:(c + 1) * block, :part].astype(jnp.bfloat16))
            return 0

        lax.fori_loop(0, n // SOURCES, unpack, 0)

    def slot_step(h, s):
        step = h * slots + s
        place = lax.rem(step, depth)
        for copy in gate_copies(step):
            copy.wait()
        gate = jnp.dot(xs[h], wg[place], preferred_element_type=jnp.float32)
        upper = jnp.dot(xs[h], wu[place], preferred_element_type=jnp.float32)

        @pl.when(step + depth < HALVES * slots)
        def _():
            for copy in gate_copies(step + depth):
                copy.start()

        if h == 0:
            gacc[s] = gate
            uacc[s] = upper
            return 0
        gate = gate + gacc[s]
        upper = upper + uacc[s]
        table = comb[...]
        lane = lax.broadcasted_iota(jnp.int32, table.shape, 1)
        scale = jnp.sum(jnp.where(lane == ep * slots + s, table, 0.0), axis=1, keepdims=True)
        hidden = gate / (1.0 + jnp.exp(-gate)) * upper
        hid[s] = (hidden * scale).astype(jnp.bfloat16)
        return 0

    middle_slot = slots // 2
    pass_on(0)
    gather(0)
    lax.fori_loop(0, middle_slot, lambda s, _: slot_step(0, s), 0)
    for i in range(ring):
        down_copy(i).start()
    pass_on(1)
    lax.fori_loop(middle_slot, slots, lambda s, _: slot_step(0, s), 0)
    gather(1)
    lax.fori_loop(0, slots, lambda s, _: slot_step(1, s), 0)

    back = order(rows, True)

    def pair_copy(h):
        return pltpu.make_async_remote_copy(
            src_ref=sbuf.at[h, other], dst_ref=pbuf.at[h], send_sem=ps_sem.at[h],
            recv_sem=pr_sem.at[h], device_id=sibling, device_id_type=MESH,
        )

    def r_copy(h, to, landed):
        return pltpu.make_async_remote_copy(
            src_ref=tbuf.at[h, to], dst_ref=rbuf.at[h, landed], send_sem=rs_sem.at[h, to],
            recv_sem=rr_sem.at[h, landed], device_id=place_of(2 * to + core), device_id_type=MESH,
        )

    def reduce_pair(h):
        pair_copy(h).wait()

        def r_send(d, _):
            to = ahead(d)
            both = sbuf[h, core, to].astype(jnp.float32) + pbuf[h, to].astype(jnp.float32)
            tbuf[h, to] = both.astype(jnp.bfloat16)
            r_copy(h, to, chip).start()
            return 0

        lax.fori_loop(1, chips, r_send, 0)

    for h in range(HALVES):
        for c in range(pieces):
            columns = slice(c * part, (c + 1) * part)
            total = None
            for s in range(slots):
                if c == 0:
                    down_copy(h * slots + s).wait()
                y = jnp.dot(hid[s], wd[(h * slots + s) % ring, :, columns],
                            preferred_element_type=jnp.float32)
                total = y if s == 0 else total + y
                later = h * slots + s + ring
                if c == pieces - 1 and later < HALVES * slots:
                    down_copy(later).start()
            if h > 0 and c == 0:
                reduce_pair(h - 1)
            ybuf[:, c] = total.astype(jnp.bfloat16).reshape(n // SOURCES, block, part)

        def pack(b, _):
            plain = ybuf[b].reshape(pieces * block, part)
            packed = jnp.dot(back, plain, preferred_element_type=jnp.float32)
            packed = packed.astype(jnp.bfloat16).reshape(2, SOURCES // 2, PACK, part)
            sbuf[h, :, pl.ds(b * (SOURCES // 2), SOURCES // 2)] = packed
            return 0

        lax.fori_loop(0, n // SOURCES, pack, 0)
        pair_copy(h).start()
    reduce_pair(HALVES - 1)

    for h in range(HALVES):
        def x_sent(d, _):
            across(h, ahead(d), me).wait_send()
            return 0

        def x_passed(d, _):
            within(h, xp[h], 2 * behind(d) + core).wait_send()
            return 0

        lax.fori_loop(1, chips, x_sent, 0)
        lax.fori_loop(0, chips, x_passed, 0)
    for h in range(HALVES):
        total = sbuf[h, core, chip].astype(jnp.float32) + pbuf[h, chip].astype(jnp.float32)

        def add(d, total):
            r_copy(h, behind(d), behind(d)).wait_recv()
            return total + rbuf[h, behind(d)].astype(jnp.float32)

        total = lax.fori_loop(1, chips, add, total)
        for c in range(pieces):
            o_ref[:, h * half + c * part:h * half + (c + 1) * part] = (
                total[c * rows:(c + 1) * rows].astype(jnp.bfloat16))

        def r_sent(d, _):
            r_copy(h, ahead(d), chip).wait_send()
            return 0

        lax.fori_loop(1, chips, r_sent, 0)


def body(tokens, expert_ids, combine_weight, slot_of_expert, w_gate, w_up, w_down):
    n_dp = lax.axis_size("dp")
    n = lax.axis_size("ep") * n_dp
    rows, width = tokens.shape
    slots, _, units = w_gate.shape
    pieces = PACK // rows
    half = width // HALVES
    part = half // pieces
    depth = min(4, HALVES * slots)
    ring = min(5, HALVES * slots)
    vmem = pl.BlockSpec(memory_space=pltpu.VMEM)
    hbm = pl.BlockSpec(memory_space=pl.ANY)
    bf16 = jnp.bfloat16
    dma = pltpu.SemaphoreType.DMA
    return pl.pallas_call(
        functools.partial(kernel, n, n_dp, rows),
        out_shape=jax.ShapeDtypeStruct((rows, width), bf16),
        in_specs=[vmem, vmem, vmem, pl.BlockSpec(memory_space=pltpu.SMEM), hbm, hbm, hbm],
        out_specs=vmem,
        scratch_shapes=[
            pltpu.VMEM((PACK, part + LANES), bf16),
            pltpu.VMEM((PACK, part), bf16),
            pltpu.VMEM((n, PACK, part + LANES), bf16),
            pltpu.VMEM((n, PACK, part), bf16),
            pltpu.VMEM((HALVES, n * rows, half), bf16),
            pltpu.VMEM((n * rows, LANES), jnp.float32),
            pltpu.VMEM((slots, n * rows, units), jnp.float32),
            pltpu.VMEM((slots, n * rows, units), jnp.float32),
            pltpu.VMEM((depth, half, units), bf16),
            pltpu.VMEM((depth, half, units), bf16),
            pltpu.VMEM((ring, units, half), bf16),
            pltpu.VMEM((slots, n * rows, units), bf16),
            pltpu.VMEM((n // SOURCES, pieces, SOURCES * rows, part), bf16),
            pltpu.VMEM((HALVES, 2, n // 2, PACK, part), bf16),
            pltpu.VMEM((HALVES, n // 2, PACK, part), bf16),
            pltpu.VMEM((HALVES, n // 2, PACK, part), bf16),
            pltpu.VMEM((HALVES, n // 2, PACK, part), bf16),
            dma((depth,)),
            dma((depth,)),
            dma((ring,)),
            dma((HALVES, n // 2)),
            dma((HALVES, n)),
            dma((HALVES, n // 2)),
            dma((HALVES,)),
            dma((HALVES,)),
            dma((HALVES, n // 2)),
            dma((HALVES, n // 2)),
        ],
        compiler_params=pltpu.CompilerParams(
            collective_id=0, has_side_effects=True, vmem_limit_bytes=60 * 2**20
        ),
        cost_estimate=pl.CostEstimate(
            flops=6 * n * rows * slots * width * units,
            bytes_accessed=6 * slots * width * units,
            transcendentals=n * rows * slots * units,
        ),
    )(tokens, expert_ids, combine_weight, slot_of_expert, w_gate, w_up, w_down)


def solution(mesh):
    in_specs = (
        P(("grp", "ep", "dp"), None),
        P(("grp", "ep", "dp"), None),
        P(("grp", "ep", "dp"), None),
        P(),
        P("ep", None, "dp"),
        P("ep", None, "dp"),
        P("ep", "dp", None),
    )
    out_specs = P(("grp", "ep", "dp"), None)
    return jax.shard_map(body, mesh=mesh, in_specs=in_specs, out_specs=out_specs, check_vma=False)
```
